128 devices in a mesh: ctx: 8 (over x, y_hi), dp: 4 (over z), shard: 4 (over y_lo, core).
Axes of the slice: x: 4, y: 4 (y_hi: 2, y_lo: 2; y = y_hi * 2 + y_lo), z: 4, core: 2. Of those that a mesh axis runs over, the one named last changes fastest.
Arguments:
- hidden_in: bfloat16 [16, 3072, 576], P(('dp', 'shard'), 'ctx'), may hold values from -6 to 6
- first_gain: bfloat16 [576], P('shard'), may hold values from 0.25 to 1.75
- query_weight: bfloat16 [576, 576], P('shard'), may hold values from -0.375 to 0.375
- key_weight: bfloat16 [576, 192], P('shard'), may hold values from -0.375 to 0.375
- value_weight: bfloat16 [576, 192], P('shard'), may hold values from -0.25 to 0.25
- output_weight: bfloat16 [576, 576], P('shard'), may hold values from -2 to 2
- second_gain: bfloat16 [576], P('shard'), may hold values from 0.25 to 1.75
- gate_weight: bfloat16 [576, 1536], P('shard'), may hold values from -0.25 to 0.25
- up_weight: bfloat16 [576, 1536], P('shard'), may hold values from -0.25 to 0.25
- down_weight: bfloat16 [1536, 576], P('shard'), may hold values from -0.15625 to 0.15625
- pair_slot: int32 [16, 8], P(('dp', 'shard')), may hold values from 0 to 7, each once within a row
- out_cotangent: bfloat16 [16, 3072, 576], P(('dp', 'shard'), 'ctx'), may hold values from -6 to 6
Outputs:
- hidden_out: bfloat16 [16, 3072, 576], P(('dp', 'shard'), 'ctx')
- grad_input: float32 [16, 3072, 576], P(('dp', 'shard'), 'ctx')
- grad_first_gain: float32 [576], P('shard')
- grad_query_weight: float32 [576, 576], P('shard')
- grad_key_weight: float32 [576, 192], P('shard')
- grad_value_weight: float32 [576, 192], P('shard')
- grad_output_weight: float32 [576, 576], P('shard')
- grad_second_gain: float32 [576], P('shard')
- grad_gate_weight: float32 [576, 1536], P('shard')
- grad_up_weight: float32 [576, 1536], P('shard')
- grad_down_weight: float32 [1536, 576], P('shard')
The draws below stay inside these ranges and needn't reach their ends.
Inputs may be any that keep to these rules, and one draw needn't show every extreme that they name: Each row of pair_slot is a permutation: cycle index c of sequence b holds the position blocks pair_slot[b, c] and 15 - pair_slot[b, c], each of half of 384 positions.
All inputs are finite; a program needn't handle non-finite values.
Results may differ from the reference program's by a relative error of at most 0.03.
Values may be sent and summed in bfloat16 or wider, within the bound.
No kernel may reach another device: no remote copies, remote signals or barrier semaphores. Data moves between devices by JAX's collectives and lax.ppermute only.
A program may use at most 128 MiB of HBM per device.

```python
import math
import jax
import jax.numpy as jnp
from jax import lax

D = 576
HEADS = 9
KV_HEADS = 3
HEAD = 64
FF = 1536
LENGTH = 3072
SPAN = 384
BATCH = 16
N_CTX = 8


def shard_levels(stream_key, shape, shards, smallest, top_value):
    loudness = 1.0
    for dim, blocks in shards:
        steps = jax.random.uniform(jax.random.fold_in(jax.random.fold_in(stream_key, 6), dim), (blocks,), jnp.float32, smallest / len(shards), top_value / len(shards))
        loudness = loudness * jnp.repeat(jnp.exp(steps), shape[dim] // blocks).reshape((-1,) + (1,) * (len(shape) - 1 - dim))
    return loudness


def noise(stream_key, extent, width, limit, split=(), kind=jnp.bfloat16):
    result = jax.random.normal(stream_key, extent, jnp.float32) * width
    if len(split) > 0:
        result = shard_levels(stream_key, extent, split, -0.22, 0.18) * result
    return jnp.clip(result, min=-limit, max=limit).astype(kind)


def setup_inputs(seed: int = 0) -> dict:
    streams_of = jax.random.split(jax.random.key(seed), 13)
    return {
        "hidden_in": noise(streams_of[0], (BATCH, LENGTH, D), 1.0, 6.0, ((0, 16), (1, 8))),
        "first_gain": jnp.clip(1.0 + 0.15 * jax.random.normal(streams_of[1], (D,), jnp.float32), 0.25, 1.75).astype(jnp.bfloat16),
        "query_weight": noise(streams_of[2], (D, HEADS * HEAD), (D // 2) ** -0.5, 0.375, ((0, 4),)),
        "key_weight": noise(streams_of[3], (D, KV_HEADS * HEAD), (D // 2) ** -0.5, 0.375, ((0, 4),)),
        "value_weight": noise(streams_of[4], (D, KV_HEADS * HEAD), D ** -0.5, 0.25, ((0, 4),)),
        "output_weight": noise(streams_of[5], (HEADS * HEAD, D), (HEADS * HEAD // 64) ** -0.5, 2.0, ((0, 4),)),
        "second_gain": jnp.clip(1.0 + 0.15 * jax.random.normal(streams_of[6], (D,), jnp.float32), 0.25, 1.75).astype(jnp.bfloat16),
        "gate_weight": noise(streams_of[7], (D, FF), D ** -0.5, 0.25, ((0, 4),)),
        "up_weight": noise(streams_of[8], (D, FF), D ** -0.5, 0.25, ((0, 4),)),
        "down_weight": noise(streams_of[9], (FF, D), FF ** -0.5, 0.15625, ((0, 4),)),
        "pair_slot": jax.vmap(lambda own: jax.random.permutation(own, N_CTX))(jax.random.split(streams_of[10], BATCH)).reshape((BATCH, N_CTX)).astype(jnp.int32),
        "out_cotangent": noise(streams_of[11], (BATCH, LENGTH, D), 1.0, 6.0, ((0, 16), (1, 8))),
    }


eps_norm = 1e-05
rope_base = 100000.0
masked_score = -1e+30
highest = lax.Precision.HIGHEST

@jax.custom_vjp
def low(v):
    return lax.optimization_barrier(v.astype(jnp.bfloat16)).astype(jnp.float32)

@jax.custom_vjp
def low_back(v):
    return v

def low_keep(v):
    return (low(v), None)

def low_pass(kept, grad):
    return (grad,)

def back_keep(v):
    return (v, None)

def back_low(kept, grad):
    return (low(grad),)
low.defvjp(low_keep, low_pass)
low_back.defvjp(back_keep, back_low)

def positions_for(rows, slots):
    device = rows // SPAN
    within = rows % SPAN
    half = SPAN // 2
    owners = jnp.arange(N_CTX, dtype=jnp.int32)
    slot = lax.optimization_barrier(jnp.sum(jnp.where(device[:, None] == owners[None, :], slots[None, :], 0), axis=1))
    block = jnp.where(within < half, slot, 2 * N_CTX - 1 - slot)
    return block * half + within % half

def rope_tables(positions):
    freqs = rope_base ** (-jnp.arange(0, HEAD, 2, dtype=jnp.float32) / HEAD)
    angles = positions.astype(jnp.float32)[:, None] * freqs[None, :]
    cosine = jnp.concatenate([jnp.cos(angles), jnp.cos(angles)], axis=-1)
    sine = jnp.concatenate([jnp.sin(angles), jnp.sin(angles)], axis=-1)
    return (cosine, sine)

def rotate(values, cosine, sine):
    half = HEAD // 2
    turned = jnp.concatenate([-values[..., half:], values[..., :half]], axis=-1)
    return values * cosine[:, None, :] + turned * sine[:, None, :]

def normalize(value, gain):
    return value * lax.rsqrt(lax.optimization_barrier(jnp.mean(value * value, axis=-1, keepdims=True)) + eps_norm) * gain

def product(left, right):
    return jnp.dot(left, right, precision=highest, preferred_element_type=jnp.float32)

def sequence_forward(hidden, slots, weights):
    gain_one, weight_query, weight_key, weight_value, weight_output, gain_two, weight_gate, weight_up, weight_down = weights
    group = HEADS // KV_HEADS
    scale = HEAD ** (-0.5)
    positions = positions_for(jnp.arange(LENGTH, dtype=jnp.int32), slots)
    cosine, sine = rope_tables(positions)
    normed_one = low(normalize(hidden, gain_one))
    query = low(rotate(low_back(product(normed_one, weight_query)).reshape(LENGTH, HEADS, HEAD), cosine, sine))
    query = query.reshape(LENGTH, KV_HEADS, group, HEAD)
    keys = low(rotate(low_back(product(normed_one, weight_key)).reshape(LENGTH, KV_HEADS, HEAD), cosine, sine))
    values = low(low_back(product(normed_one, weight_value))).reshape(LENGTH, KV_HEADS, HEAD)
    rows_block = math.gcd(LENGTH, 512)

    def attend(start):
        query_rows = lax.dynamic_slice_in_dim(query, start, rows_block, 0)
        query_place = lax.dynamic_slice_in_dim(positions, start, rows_block, 0)
        scores = low_back(jnp.einsum('qhgd,khd->qhgk', query_rows, keys, precision=highest) * scale)
        allowed = (positions[None, :] <= query_place[:, None])[:, None, None, :]
        masked = jnp.where(allowed, scores, masked_score)
        peak = lax.optimization_barrier(jnp.max(masked, axis=-1, keepdims=True))
        raised = jnp.where(allowed, jnp.exp(masked - peak), 0.0)
        total = lax.optimization_barrier(jnp.sum(raised, axis=-1, keepdims=True))
        return jnp.einsum('qhgk,khd->qhgd', low(raised), values, precision=highest) / total
    starts = jnp.arange(0, LENGTH, rows_block, dtype=jnp.int32)
    mixed = lax.map(jax.checkpoint(attend), starts).reshape(LENGTH, HEADS * HEAD)
    attended = low(low_back(mixed))
    middle = hidden + low_back(product(attended, weight_output))
    normed_two = low(normalize(middle, gain_two))
    gate = low_back(product(normed_two, weight_gate))
    lifted = low_back(product(normed_two, weight_up))
    activated = low(jax.nn.silu(gate) * lifted)
    return middle + low_back(product(activated, weight_down))

def reference(hidden_in, first_gain, query_weight, key_weight, value_weight, output_weight, second_gain, gate_weight, up_weight, down_weight, pair_slot, out_cotangent):
    weights = tuple((array.astype(jnp.float32) for array in (first_gain, query_weight, key_weight, value_weight, output_weight, second_gain, gate_weight, up_weight, down_weight)))

    def forward(hidden, params):

        def single(pair):
            return jax.checkpoint(sequence_forward)(pair[0], pair[1], params)
        return lax.map(single, (hidden, pair_slot))
    outputs, pullback = jax.vjp(forward, hidden_in.astype(jnp.float32), weights)
    grad_hidden, grad_weights = pullback(out_cotangent.astype(jnp.float32))
    return (outputs.astype(jnp.bfloat16), grad_hidden, grad_weights[0], grad_weights[1], grad_weights[2], grad_weights[3], grad_weights[4], grad_weights[5], grad_weights[6], grad_weights[7], grad_weights[8])
```

```python
import functools

import jax
import jax.numpy as jnp
from jax import lax
from jax.experimental import pallas as pl
from jax.experimental.pallas import tpu as pltpu
from jax.sharding import PartitionSpec as P

HEADS = 9
KV_HEADS = 3
GROUP = 3
HEAD = 64
WIDTH = 576
FF = 1536
SPAN = 384
HALF = 192
CYCLE = 8
BLOCKS = 2 * CYCLE
QUERIES = 640
LANES = 128
ROWS = 144
EARLY = 6144
CHUNK = EARLY // 4
MIDDLE = 768
LATE = 448
TAIL = 448
REST = 3 * FF + WIDTH + 64

eps_norm = 1e-05
rope_base = 100000.0
masked_score = -1e30
bf16 = jnp.bfloat16
f32 = jnp.float32
AXES = ("ctx", "dp", "shard")
VMEM_LIMIT = 56 * 1024 * 1024
SMEM = pl.BlockSpec(memory_space=pltpu.SMEM)
VMEM = pl.BlockSpec(memory_space=pltpu.VMEM)


def move(block, dx=0, dy=0, dz=0, dc=0):
    route = []
    for x in range(4):
        for y in range(4):
            for z in range(4):
                for core in range(2):
                    ends = []
                    for a, b, c, d in (
                        (x, y, z, core),
                        ((x + dx) % 4, (y + dy) % 4, (z + dz) % 4, (core + dc) % 2),
                    ):
                        ends.append(((a * 2 + b // 2) * 4 + c) * 4 + (b % 2) * 2 + d)
                    route.append(tuple(ends))
    return lax.ppermute(block, AXES, route)


def dot(left, right, dims):
    return lax.dot_general(left, right, (dims, ((), ())), preferred_element_type=f32)


NN = ((1,), (0,))
NT = ((1,), (1,))


def turned(array):
    return array.astype(f32).T.astype(bf16)


def lane_of(shape):
    return lax.broadcasted_iota(jnp.int32, shape, 1)


def tile_of(index):
    return slice(index * LANES, (index + 1) * LANES)


def swapped_halves(tile):
    lane = lane_of(tile.shape)
    return jnp.where(lane % HEAD < HEAD // 2, pltpu.roll(tile, LANES - 32, 1), pltpu.roll(tile, 32, 1))


def fetch_pair(first, second):
    first_other = move(first, dy=1)
    second_other = move(second, dy=-1)
    return (
        first, move(first, dc=1), first_other, move(first_other, dc=1),
        second, move(second, dc=1), second_other, move(second_other, dc=1),
    )


def spread_shards(me, parts, out, cut):
    own, low, high, core_own, core_low, core_high = parts
    out[me] = own[...]
    out[me ^ 1] = core_own[...]
    out[me ^ 2, :, :cut] = low[...]
    out[me ^ 2, :, cut:] = high[...]
    out[me ^ 3, :, :cut] = core_low[...]
    out[me ^ 3, :, cut:] = core_high[...]


def fetch_shards(own, cut):
    low = move(own[:, :cut], dy=1)
    high = move(own[:, cut:], dy=-1)
    return own, low, high, move(own, dc=1), move(low, dc=1), move(high, dc=1)


def project_kernel(info, hidden_ref, *refs):
    parts, (cos_ref, sin_ref, normed_ref, query_ref, kv_ref, weight_ref, gains_ref, tails) = refs[:8], refs[8:]
    me = info[BLOCKS + 1]
    for index in range(4):
        weight_ref[me ^ index, :, :WIDTH] = parts[index][...]
        tails[me ^ index] = parts[4 + index][...]
    tail = tails[...].reshape(WIDTH, TAIL).astype(f32)
    gains = tail[:, 3 * LANES :].T
    gains_ref[0] = gains[0:1]
    gains_ref[1] = gains[32:33]
    weight_ref[:, :, WIDTH:QUERIES] = jnp.zeros((4, ROWS, HEAD), bf16)
    for head in range(KV_HEADS):
        both = [tail[:, start : start + HEAD] for start in (head * HEAD, (KV_HEADS + head) * HEAD)]
        weight_ref[:, :, tile_of(5 + head)] = jnp.concatenate(both, 1).astype(bf16).reshape(4, ROWS, LANES)
    hidden = hidden_ref[...].astype(f32).T
    inverse = lax.rsqrt(jnp.mean(hidden * hidden, axis=-1, keepdims=True) + eps_norm)
    normed = (hidden * inverse * gains[0:1]).astype(bf16)
    normed_ref[...] = normed
    cosine = cos_ref[...]
    sine = sin_ref[...]
    first = lane_of((SPAN, LANES)) < HEAD
    for tile in range(8):
        raw = dot(normed, weight_ref[:, :, tile_of(tile)].reshape(WIDTH, LANES), NN)
        roped = raw * cosine + swapped_halves(raw) * sine
        if tile < 5:
            roped = roped * (HEAD**-0.5)
            query_ref[:, tile_of(2 * tile)] = jnp.where(first, roped, 0.0).astype(bf16)
            if tile < 4:
                query_ref[:, tile_of(2 * tile + 1)] = jnp.where(first, pltpu.roll(roped, HEAD, 1), 0.0).astype(bf16)
        else:
            kv_ref[:, tile_of(tile - 5)] = jnp.where(first, roped, raw).astype(bf16)


def project(info, hidden, parts, cosine, sine):
    return pl.pallas_call(
        project_kernel,
        out_shape=(
            jax.ShapeDtypeStruct((SPAN, WIDTH), bf16),
            jax.ShapeDtypeStruct((SPAN, HEADS * LANES), bf16),
            jax.ShapeDtypeStruct((SPAN, KV_HEADS * LANES), bf16),
            jax.ShapeDtypeStruct((4, ROWS, 1024), bf16),
            jax.ShapeDtypeStruct((2, 1, WIDTH), f32),
        ),
        in_specs=[SMEM] + [VMEM] * 11,
        scratch_shapes=[pltpu.VMEM((4, ROWS, TAIL), bf16)],
        compiler_params=pltpu.CompilerParams(vmem_limit_bytes=VMEM_LIMIT),
        cost_estimate=pl.CostEstimate(flops=2 * SPAN * WIDTH * 1024, bytes_accessed=4 << 20, transcendentals=0),
        name="project",
    )(info, hidden, *parts, cosine, sine)


def stacked_heads(ref, half, group):
    return jnp.concatenate(
        [ref[half * HALF : (half + 1) * HALF, tile_of(group * GROUP + head)] for head in range(GROUP)]
        + [jnp.zeros((QUERIES - GROUP * HALF, LANES), ref.dtype)],
        axis=0,
    )


def allowed_pairs():
    shape = (HALF, QUERIES)
    return lax.broadcasted_iota(jnp.int32, shape, 0) <= lane_of(shape) % HALF


def attend_kernel(info, query_ref, *refs):
    kv_parts, (mixed_ref, log_ref, kv_ref), scratch = refs[:10], refs[10:13], refs[13:]
    for index in range(6):
        for half in range(2):
            kv_ref[2 * index + half] = kv_parts[index][half * HALF : (half + 1) * HALF]
    for half in range(4):
        kv_ref[12 + half] = kv_parts[6 + half][...]
    query, summed, peak, total = (scratch[3 * i : 3 * i + 3] for i in range(4))
    groups = range(KV_HEADS)
    high = lane_of((QUERIES, LANES)) >= HEAD
    for half in range(2):
        for group in groups:
            query[group][...] = turned(stacked_heads(query_ref, half, group))
            summed[group][...] = jnp.zeros((HEAD, QUERIES), f32)
            peak[group][...] = jnp.full((1, QUERIES), masked_score, f32)
            total[group][...] = jnp.zeros((1, QUERIES), f32)

        def visit(place, diagonal):
            blocks = [kv_ref[place, :, tile_of(group)] for group in groups]
            scores = [dot(blocks[group], query[group][...], NN) for group in groups]
            for group in groups:
                masked = jnp.where(allowed_pairs(), scores[group], masked_score) if diagonal else scores[group]
                old_peak = peak[group][...]
                new_peak = jnp.maximum(old_peak, jnp.max(masked, axis=0, keepdims=True))
                raised = jnp.exp(masked - new_peak)
                factor = jnp.exp(old_peak - new_peak)
                peak[group][...] = new_peak
                total[group][...] = total[group][...] * factor + jnp.sum(raised, axis=0, keepdims=True)
                product = dot(turned(blocks[group])[HEAD:], raised.astype(bf16), NN)
                summed[group][...] = summed[group][...] * factor + product

        def step(index, carry):
            visit(info[index], False)
            return carry

        last = info[BLOCKS] if half == 0 else 2 * CYCLE - 1 - info[BLOCKS]
        lax.fori_loop(0, last, step, 0)
        visit(info[last], True)
        for group in groups:
            mixed = summed[group][...] / total[group][...]
            upright = jnp.concatenate([jnp.zeros((HEAD, QUERIES), f32), mixed], 0).T
            log_ref[half, group] = peak[group][...] + jnp.log(total[group][...])
            for head in range(GROUP):
                mixed_ref[half * HALF : (half + 1) * HALF, tile_of(group * GROUP + head)] = upright[
                    head * HALF : (head + 1) * HALF
                ]


def attend(info, query, kv_parts):
    return pl.pallas_call(
        attend_kernel,
        out_shape=(
            jax.ShapeDtypeStruct((SPAN, HEADS * LANES), f32),
            jax.ShapeDtypeStruct((2, KV_HEADS, 1, QUERIES), f32),
            jax.ShapeDtypeStruct((BLOCKS, HALF, KV_HEADS * LANES), bf16),
        ),
        in_specs=[SMEM] + [VMEM] * 11,
        scratch_shapes=[pltpu.VMEM((LANES, QUERIES), bf16)] * 3
        + [pltpu.VMEM((HEAD, QUERIES), f32)] * 3
        + [pltpu.VMEM((1, QUERIES), f32)] * 6,
        compiler_params=pltpu.CompilerParams(vmem_limit_bytes=VMEM_LIMIT),
        cost_estimate=pl.CostEstimate(flops=20 << 30, bytes_accessed=8 << 20, transcendentals=17 * HALF * QUERIES * 3),
        name="attend",
    )(info, query, *kv_parts)


def attend_back_kernel(
    info, query_ref, kv_ref, mixed_ref, mixed_grad_ref, log_ref, cos_ref, sin_ref, query_grad_ref, kv_grad_ref, *scratch
):
    query, query_t, grads, grads_t, query_sum, kv_sum, delta, log_total = (
        scratch[3 * i : 3 * i + 3] for i in range(8)
    )
    groups = range(KV_HEADS)
    for group in groups:
        kv_sum[group][...] = jnp.zeros((BLOCKS, HALF, LANES), f32)
    first = lane_of((HALF, LANES)) < HEAD
    for half in range(2):
        rows = slice(half * HALF, (half + 1) * HALF)
        for group in groups:
            stacked = stacked_heads(query_ref, half, group)
            query[group][...] = stacked
            query_t[group][...] = turned(stacked)
            stacked = stacked_heads(mixed_grad_ref, half, group)
            grads[group][...] = stacked
            grads_t[group][...] = turned(stacked)
            terms = stacked.astype(f32) * stacked_heads(mixed_ref, half, group)
            delta[group][...] = jnp.sum(terms.T, axis=0, keepdims=True)
            log_total[group][...] = log_ref[half, group]
            query_sum[group][...] = jnp.zeros((HEAD, QUERIES), f32)

        def visit(place, diagonal):
            blocks = [kv_ref[place, :, tile_of(group)] for group in groups]
            scores = [dot(blocks[group], query_t[group][...], NN) for group in groups]
            chance_grads = [dot(blocks[group], grads_t[group][...], NN) for group in groups]
            for group in groups:
                masked = jnp.where(allowed_pairs(), scores[group], masked_score) if diagonal else scores[group]
                chance = jnp.exp(masked - log_total[group][...])
                score_grad = (chance * (chance_grads[group] - delta[group][...])).astype(bf16)
                kv_sum[group][place] += dot(chance.astype(bf16), grads[group][...], NN) + dot(
                    score_grad, query[group][...], NN
                )
                query_sum[group][...] += dot(turned(blocks[group])[:HEAD], score_grad, NN)

        def step(index, carry):
            visit(info[index], False)
            return carry

        last = info[BLOCKS] if half == 0 else 2 * CYCLE - 1 - info[BLOCKS]
        lax.fori_loop(0, last, step, 0)
        visit(info[last], True)
        cosine = cos_ref[rows, :]
        sine = sin_ref[rows, :]
        for group in groups:
            upright = jnp.concatenate([query_sum[group][...], jnp.zeros((HEAD, QUERIES), f32)], 0).T
            for head in range(GROUP):
                tile = upright[head * HALF : (head + 1) * HALF] * (HEAD**-0.5)
                tile = tile * cosine - swapped_halves(tile) * sine
                query_grad_ref[rows, tile_of(group * GROUP + head)] = jnp.where(first, tile, 0.0).astype(bf16)
    for group in groups:
        kv_grad_ref[:, :, tile_of(group)] = kv_sum[group][...].astype(bf16)


def attend_back(info, query, kv, mixed, mixed_grad, log_total, cosine, sine):
    return pl.pallas_call(
        attend_back_kernel,
        out_shape=(
            jax.ShapeDtypeStruct((SPAN, HEADS * LANES), bf16),
            jax.ShapeDtypeStruct((BLOCKS, HALF, KV_HEADS * LANES), bf16),
        ),
        in_specs=[SMEM] + [VMEM] * 7,
        scratch_shapes=(
            [pltpu.VMEM((QUERIES, LANES), bf16)] * 3
            + [pltpu.VMEM((LANES, QUERIES), bf16)] * 3
            + [pltpu.VMEM((QUERIES, LANES), bf16)] * 3
            + [pltpu.VMEM((LANES, QUERIES), bf16)] * 3
            + [pltpu.VMEM((HEAD, QUERIES), f32)] * 3
            + [pltpu.VMEM((BLOCKS, HALF, LANES), f32)] * 3
            + [pltpu.VMEM((1, QUERIES), f32)] * 6
        ),
        compiler_params=pltpu.CompilerParams(vmem_limit_bytes=VMEM_LIMIT),
        cost_estimate=pl.CostEstimate(flops=40 << 30, bytes_accessed=12 << 20, transcendentals=17 * HALF * QUERIES * 3),
        name="attend_back",
    )(info, query, kv, mixed, mixed_grad, log_total, cosine, sine)


def feed_kernel(
    info, hidden_ref, cotangent_ref, mixed_ref, gains_ref, own, low, high, core_own, core_low, core_high,
    out_ref, middle_grad_ref, mixed_grad_ref, gain_grad_ref, keep_ref, away_ref, weight, grads_t, down, normed_t, attended_t,
):
    spread_shards(info[BLOCKS + 1], (own, low, high, core_own, core_low, core_high), weight, FF + FF)
    core = info[BLOCKS + 2]
    gain = gains_ref[1]

    def columns(start, width):
        return weight[:, :, start : start + width].reshape(WIDTH, width)

    weight_output = columns(3 * FF, WIDTH)
    for shard in range(4):
        for part in range(4):
            start = 2 * FF + part * SPAN
            down[part * ROWS : (part + 1) * ROWS, shard * SPAN : (shard + 1) * SPAN] = weight[shard, :, start : start + SPAN]

    def store(ref, y, start, value):
        done = 0
        while done < value.shape[0]:
            chunk, within = divmod(start + done, CHUNK)
            count = min(value.shape[0] - done, CHUNK - within)
            ref[chunk, y, within : within + count, :] = value[done : done + count, :]
            done += count

    def store_ordered(tile, value):
        for k in range(4):
            store(keep_ref if k < 2 else away_ref, k % 2, tile * ROWS, value[k * ROWS : (k + 1) * ROWS, :])

    tiles = []
    for tile in range(5):
        joined = pltpu.roll(mixed_ref[:, tile_of(2 * tile)], HEAD, 1)
        if tile < 4:
            joined = joined + mixed_ref[:, tile_of(2 * tile + 1)]
        tiles.append(joined)
    attended = jnp.concatenate(tiles, 1)
    attended_t[...] = attended.T.astype(bf16)
    attended = attended[:, :WIDTH].astype(bf16)
    middle = hidden_ref[...].astype(f32).T + dot(attended, weight_output, NN)
    inverse = lax.rsqrt(jnp.mean(middle * middle, axis=-1, keepdims=True) + eps_norm)
    normed_wide = middle * inverse * gain
    normed = normed_wide.astype(bf16)
    normed_t[...] = normed_wide.T.astype(bf16)

    def keep_first(ref):
        starts = [(2 * (k % 2) + (core if k < 2 else 1 - core)) * ROWS for k in range(4)]
        return jnp.concatenate([ref[pl.ds(pl.multiple_of(start, 16), ROWS), :] for start in starts], 0)

    normed_rows = keep_first(normed_t)
    attended_rows = keep_first(attended_t)
    cotangent_t = cotangent_ref[...]
    grads_t[...] = turned(cotangent_t)
    branch_grad = grads_t[...]

    total = middle
    normed_grad = jnp.zeros((SPAN, WIDTH), f32)
    for part in range(3):
        weight_gate = columns(part * 512, 512)
        weight_up = columns(FF + part * 512, 512)
        weight_down = down[:, part * 512 : (part + 1) * 512]
        gate = dot(normed, weight_gate, NN)
        lifted = dot(normed, weight_up, NN)
        act_grad = dot(branch_grad, weight_down, NN)
        sigmoid = 1.0 / (1.0 + jnp.exp(-gate))
        swish = gate * sigmoid
        activated = (swish * lifted).astype(bf16)
        total = total + dot(activated, weight_down, NT)
        gate_grad = (act_grad * lifted * sigmoid * (1.0 + gate * (1.0 - sigmoid))).astype(bf16)
        lifted_grad = (act_grad * swish).astype(bf16)
        normed_grad = normed_grad + dot(gate_grad, weight_gate, NT) + dot(lifted_grad, weight_up, NT)
        for base, upper in ((0, gate_grad), (12, lifted_grad)):
            grad = dot(normed_rows, upper, NN).astype(bf16)
            for tile in range(4):
                store_ordered(base + 4 * part + tile, grad[:, tile_of(tile)])
        grad = dot(cotangent_t, activated, NN).astype(bf16)
        for tile in range(4):
            shard, within = divmod(4 * part + tile, 3)
            for ref, here in ((keep_ref, core == shard % 2), (away_ref, core != shard % 2)):

                @pl.when(here)
                def _(ref=ref):
                    store(ref, shard // 2, 24 * ROWS + within * WIDTH, grad[:, tile_of(tile)])

    out_ref[...] = total.T.astype(bf16)
    scaled = normed_grad * gain
    gain_grad_ref[...] = jnp.sum(normed_grad * middle * inverse, axis=0, keepdims=True)
    middle_grad = (
        branch_grad.astype(f32)
        + inverse * scaled
        - inverse * inverse * inverse * middle * jnp.mean(scaled * middle, axis=-1, keepdims=True)
    )
    middle_grad_ref[...] = middle_grad
    block_grad = middle_grad.astype(bf16)
    grad = dot(attended_rows, block_grad, NN).astype(bf16)
    grad = jnp.concatenate([grad, jnp.zeros((WIDTH, 64), bf16)], 1)
    for tile in range(5):
        store_ordered(36 + tile, grad[:, tile_of(tile)])
    for ref in (keep_ref, away_ref):
        ref[3, :, 41 * ROWS - 3 * CHUNK :, :] = jnp.zeros((2, EARLY - 41 * ROWS, LANES), bf16)
    mixed_grad = dot(block_grad, weight_output, NT)
    mixed_grad = jnp.concatenate([mixed_grad, jnp.zeros((SPAN, 64), f32)], 1)
    second = lane_of((SPAN, LANES)) >= HEAD
    for tile in range(5):
        both = mixed_grad[:, tile_of(tile)]
        mixed_grad_ref[:, tile_of(2 * tile)] = jnp.where(second, pltpu.roll(both, HEAD, 1), 0.0).astype(bf16)
        if tile < 4:
            mixed_grad_ref[:, tile_of(2 * tile + 1)] = jnp.where(second, both, 0.0).astype(bf16)


def feed(info, hidden, cotangent, mixed, gains, parts):
    return pl.pallas_call(
        feed_kernel,
        out_shape=(
            jax.ShapeDtypeStruct((WIDTH, SPAN), bf16),
            jax.ShapeDtypeStruct((SPAN, WIDTH), f32),
            jax.ShapeDtypeStruct((SPAN, HEADS * LANES), bf16),
            jax.ShapeDtypeStruct((1, WIDTH), f32),
            jax.ShapeDtypeStruct((4, 2, CHUNK, LANES), bf16),
            jax.ShapeDtypeStruct((4, 2, CHUNK, LANES), bf16),
        ),
        in_specs=[SMEM] + [VMEM] * 10,
        scratch_shapes=[
            pltpu.VMEM((4, ROWS, REST), bf16),
            pltpu.VMEM((SPAN, WIDTH), bf16),
            pltpu.VMEM((WIDTH, FF), bf16),
            pltpu.VMEM((WIDTH, SPAN), bf16),
            pltpu.VMEM((QUERIES, SPAN), bf16),
        ],
        compiler_params=pltpu.CompilerParams(vmem_limit_bytes=VMEM_LIMIT),
        cost_estimate=pl.CostEstimate(flops=8 << 30, bytes_accessed=20 << 20, transcendentals=SPAN * FF),
        name="feed",
    )(info, hidden, cotangent, mixed, gains, *parts)


def store_grads(ref, normed_t, before, tiles):
    for tile in range(tiles):
        part = dot(normed_t, before[:, tile_of(tile)], NN).astype(bf16)
        for shard in range(4):
            ref[shard, tile * ROWS : (tile + 1) * ROWS, :] = part[shard * ROWS : (shard + 1) * ROWS, :]


def query_back_kernel(query_grad_ref, normed_ref, weight_ref, weight_grad_ref, normed_grad_ref, pre):
    for tile in range(5):
        joined = query_grad_ref[:, tile_of(2 * tile)].astype(f32)
        if tile < 4:
            joined = joined + pltpu.roll(query_grad_ref[:, tile_of(2 * tile + 1)].astype(f32), HEAD, 1)
        pre[:, tile_of(tile)] = joined.astype(bf16)
    before = pre[...]
    store_grads(weight_grad_ref, turned(normed_ref[...]), before, 5)
    weight_grad_ref[:, 5 * ROWS :, :] = jnp.zeros((4, MIDDLE - 5 * ROWS, LANES), bf16)
    normed_grad_ref[...] = dot(before, weight_ref[:, :, :QUERIES].reshape(WIDTH, QUERIES), NT)


def query_back(query_grad, normed, weight):
    return pl.pallas_call(
        query_back_kernel,
        out_shape=(
            jax.ShapeDtypeStruct((4, MIDDLE, LANES), bf16),
            jax.ShapeDtypeStruct((SPAN, WIDTH), f32),
        ),
        in_specs=[VMEM] * 3,
        scratch_shapes=[pltpu.VMEM((SPAN, QUERIES), bf16)],
        compiler_params=pltpu.CompilerParams(vmem_limit_bytes=VMEM_LIMIT),
        cost_estimate=pl.CostEstimate(flops=4 * SPAN * WIDTH * QUERIES, bytes_accessed=4 << 20, transcendentals=0),
        name="query_back",
    )(query_grad, normed, weight)


def finish_kernel(
    kv_sum_ref, normed_ref, weight_ref, hidden_ref, gains_ref, middle_grad_ref, normed_grad_ref, gain_grad_ref,
    cos_ref, sin_ref, weight_grad_ref, input_grad_ref, pre,
):
    cosine = cos_ref[...]
    sine = sin_ref[...]
    first = lane_of((SPAN, LANES)) < HEAD
    for tile in range(3):
        raw = kv_sum_ref[:, tile_of(tile)]
        back = raw * cosine - swapped_halves(raw) * sine
        pre[:, tile_of(tile)] = jnp.where(first, back, raw).astype(bf16)
    before = pre[...]
    store_grads(weight_grad_ref, turned(normed_ref[...]), before, 3)
    normed_grad = normed_grad_ref[...] + dot(before, weight_ref[:, :, QUERIES:].reshape(WIDTH, 3 * LANES), NT)
    hidden = hidden_ref[...].astype(f32).T
    inverse = lax.rsqrt(jnp.mean(hidden * hidden, axis=-1, keepdims=True) + eps_norm)
    scaled = normed_grad * gains_ref[0]
    first_gain_grad = jnp.sum(normed_grad * hidden * inverse, axis=0, keepdims=True)
    gain_grads = jnp.concatenate([first_gain_grad, gain_grad_ref[...]], 0)
    gain_grads = jnp.concatenate([gain_grads, jnp.zeros((2, WIDTH), f32)], 0)
    weight_grad_ref[:, 3 * ROWS :, :] = jnp.zeros((4, LATE - 3 * ROWS, LANES), bf16)
    for shard in range(4):
        part = gain_grads[:, shard * ROWS : (shard + 1) * ROWS]
        rest = jnp.concatenate([part[:, LANES:], jnp.zeros((4, LANES - (ROWS - LANES)), f32)], 1)
        rows = jnp.concatenate([part[:, :LANES], rest, jnp.zeros((8, LANES), f32)], 0)
        weight_grad_ref[shard, 3 * ROWS : 3 * ROWS + 16, :] = rows.astype(bf16)
    input_grad = (
        middle_grad_ref[...]
        + inverse * scaled
        - inverse * inverse * inverse * hidden * jnp.mean(scaled * hidden, axis=-1, keepdims=True)
    )
    input_grad_ref[...] = input_grad.T


def finish(*operands):
    return pl.pallas_call(
        finish_kernel,
        out_shape=(
            jax.ShapeDtypeStruct((4, LATE, LANES), bf16),
            jax.ShapeDtypeStruct((WIDTH, SPAN), f32),
        ),
        in_specs=[VMEM] * 10,
        scratch_shapes=[pltpu.VMEM((SPAN, 3 * LANES), bf16)],
        compiler_params=pltpu.CompilerParams(vmem_limit_bytes=VMEM_LIMIT),
        cost_estimate=pl.CostEstimate(flops=4 * SPAN * WIDTH * SPAN, bytes_accessed=8 << 20, transcendentals=0),
        name="finish",
    )(*operands)


def total_of(*blocks):
    total = blocks[0].astype(f32)
    for block in blocks[1:]:
        total = total + block.astype(f32)
    return total.astype(bf16)


def four_ahead(array, dim, here):
    size = array.shape[dim] // 4
    return [lax.dynamic_slice_in_dim(array, ((here + step) % 4) * size, size, dim) for step in range(4)]


def send_ahead(blocks, axis):
    return [move(blocks[step], **{axis: step}) for step in (1, 3, 2)]


def send_over_y(own, other):
    return [move(other, dy=1), move(other, dy=3), move(own, dy=2)]


def in_order(own, arrived, here):
    before, after, far = arrived
    around = jnp.stack([own, after, far, before], 0)
    return jnp.concatenate([lax.dynamic_slice_in_dim(around, (step - here) % 4, 1, 0) for step in range(4)], 0)


def part_of(rows, dim, index):
    return lax.dynamic_slice_in_dim(rows, index, 1, dim).reshape(rows.shape[:dim] + rows.shape[dim + 1 :])


def unpack_kernel(
    info, own, before, after, far_low, far_high, late,
    gate_ref, up_ref, down_ref, output_ref, query_ref, key_ref, value_ref, gains_ref, rows,
):
    z = info[BLOCKS + 3]
    half = far_low.shape[0]
    rows[z] = own[...]
    rows[(z + 3) % 4] = before[...]
    rows[(z + 1) % 4] = after[...]
    rows[(z + 2) % 4, :half] = far_low[...]
    rows[(z + 2) % 4, half:] = far_high[...]

    def fetch(start, count, size=CHUNK, base=0):
        parts = []
        while count:
            chunk, within = divmod(start, size)
            taken = min(count, size - within)
            parts.append(rows[chunk, base + within : base + within + taken, :].astype(f32))
            start, count = start + taken, count - taken
        return jnp.concatenate(parts, 0)

    for tile in range(12):
        gate_ref[:, tile_of(tile)] = fetch(tile * ROWS, ROWS)
        up_ref[:, tile_of(tile)] = fetch((12 + tile) * ROWS, ROWS)
    for tile in range(3):
        down_ref[:, tile_of(tile)] = fetch(24 * ROWS + tile * WIDTH, WIDTH)
    for tile in range(5):
        columns = slice(tile * LANES, min((tile + 1) * LANES, WIDTH))
        width = columns.stop - columns.start
        output_ref[:, columns] = fetch((36 + tile) * ROWS, ROWS)[:, :width]
        query_ref[:, columns] = fetch(tile * ROWS, ROWS, MIDDLE // 4, CHUNK)[:, :width]
    for head in range(KV_HEADS):
        both = late[head * ROWS : (head + 1) * ROWS, :].astype(f32)
        key_ref[:, head * HEAD : (head + 1) * HEAD] = both[:, :HEAD]
        value_ref[:, head * HEAD : (head + 1) * HEAD] = both[:, HEAD:]
    gains = late[3 * ROWS :, :].astype(f32)
    for index in range(2):
        gains_ref[index : index + 1, :LANES] = gains[index : index + 1]
        gains_ref[index : index + 1, LANES:] = gains[4 + index : 5 + index, : ROWS - LANES]


def unpack(*operands):
    shapes = ((ROWS, FF), (ROWS, FF), (WIDTH, SPAN), (ROWS, WIDTH), (ROWS, WIDTH), (ROWS, 192), (ROWS, 192), (2, ROWS))
    return pl.pallas_call(
        unpack_kernel,
        out_shape=tuple(jax.ShapeDtypeStruct(shape, f32) for shape in shapes),
        in_specs=[SMEM] + [VMEM] * 6,
        scratch_shapes=[pltpu.VMEM((4, CHUNK + MIDDLE // 4, LANES), bf16)],
        compiler_params=pltpu.CompilerParams(vmem_limit_bytes=VMEM_LIMIT),
        cost_estimate=pl.CostEstimate(flops=0, bytes_accessed=6 << 20, transcendentals=0),
        name="unpack",
    )(*operands)


def body(
    hidden_in,
    first_gain,
    query_weight,
    key_weight,
    value_weight,
    output_weight,
    second_gain,
    gate_weight,
    up_weight,
    down_weight,
    pair_slot,
    out_cotangent,
):
    cycle_index = lax.axis_index("ctx")
    x = cycle_index // 2
    y_hi = cycle_index % 2
    z = lax.axis_index("dp")
    me = lax.axis_index("shard")
    y_lo = me // 2
    core = me % 2
    slots = pair_slot[0]

    gains = jnp.concatenate(
        [jnp.broadcast_to(first_gain[:, None], (ROWS, 32)), jnp.broadcast_to(second_gain[:, None], (ROWS, 32))], 1
    )
    packed = fetch_pair(query_weight, jnp.concatenate([key_weight, value_weight, gains], 1))

    owners = jnp.arange(CYCLE, dtype=jnp.int32)
    slot = jnp.sum(jnp.where(owners == cycle_index, slots, 0))
    row = lax.broadcasted_iota(jnp.int32, (SPAN, LANES), 0)
    lane = lax.broadcasted_iota(jnp.int32, (SPAN, LANES), 1)
    place = jnp.where(row < HALF, slot, 2 * CYCLE - 1 - slot) * HALF + row % HALF
    freqs = rope_base ** (-(2 * (jnp.arange(LANES) % 32)).astype(f32) / HEAD)
    angles = place.astype(f32) * freqs[None, :]
    cosine = jnp.cos(angles)
    sine = jnp.where(lane % HEAD < HEAD // 2, -1.0, 1.0) * jnp.sin(angles)

    steps = jnp.array([0, 0, 3, 3, 1, 1, 2, 2], jnp.int32)
    there = ((x + steps) % 4) * 2 + (y_hi + owners) % 2
    found = jnp.sum(jnp.where(there[:, None] == owners[None, :], slots[None, :], 0), 1)
    order = jnp.arange(BLOCKS, dtype=jnp.int32)
    where_found = jnp.sum(
        jnp.where(found[None, :] == order[:, None], 2 * owners[None, :], 0)
        + jnp.where(BLOCKS - 1 - found[None, :] == order[:, None], 2 * owners[None, :] + 1, 0),
        1,
    )
    info = jnp.concatenate([where_found, slot[None], me[None], core[None], z[None]]).astype(jnp.int32)

    hidden = hidden_in[0].T
    cotangent = out_cotangent[0].T
    normed_one, query, kv_own, weight_one, gains = project(info, hidden, packed, cosine, sine)

    partner = move(kv_own, dy=2)
    left = move(kv_own, dx=1)
    right = move(kv_own, dx=-1)
    rest = jnp.concatenate(
        [gate_weight, up_weight, down_weight.T.reshape(4, ROWS, SPAN)[0]]
        + [down_weight.T.reshape(4, ROWS, SPAN)[part] for part in (1, 2, 3)]
        + [output_weight, jnp.zeros((ROWS, 64), bf16)],
        1,
    )
    rest, partner, left, right = lax.optimization_barrier((rest, partner, left, right))
    rest = fetch_shards(rest, FF + FF)
    left_partner = move(partner, dx=1)
    right_partner = move(partner, dx=-1)
    far = [move(left[:HALF], dx=1), move(right[HALF:], dx=-1)]
    far_partner = [move(left_partner[:HALF], dx=1), move(right_partner[HALF:], dx=-1)]
    mixed, log_total, kv = attend(
        info, query, [kv_own, partner, left, left_partner, right, right_partner] + far + far_partner
    )
    hidden_out, middle_grad, mixed_grad, grad_gain_two, keep, away = feed(info, hidden, cotangent, mixed, gains, rest)
    got = move(away, dc=1)

    query_grad, kv_grad = attend_back(info, query, kv, mixed, mixed_grad, log_total, cosine, sine)
    kv_grad = kv_grad.reshape(4, 2, SPAN, KV_HEADS * LANES)
    far_low, far_high = kv_grad[3, :, :HALF], kv_grad[3, :, HALF:]
    far_low, far_high, query_grad = lax.optimization_barrier((far_low, far_high, query_grad))
    from_left = move(far_low, dx=1)
    from_right = move(far_high, dx=-1)

    early, query_grad = lax.optimization_barrier((total_of(keep, got), query_grad))
    early = lax.psum_scatter(early, "dp", scatter_dimension=0, tiled=False)
    grad_query, normed_grad = query_back(query_grad, normed_one, weight_one)
    grad_query = grad_query.reshape(2, 2, MIDDLE, LANES)
    middle_got = move(part_of(grad_query, 1, 1 - core), dc=1)

    to_left = jnp.concatenate([kv_grad[1, :, :HALF], kv_grad[1, :, HALF:] + from_right], 1)
    to_right = jnp.concatenate([kv_grad[2, :, :HALF] + from_left, kv_grad[2, :, HALF:]], 1)
    to_left, to_right, middle_got = lax.optimization_barrier((to_left, to_right, middle_got))
    kv_arrived = move(to_right, dx=1), move(to_left, dx=-1)
    middle_rows = four_ahead(total_of(part_of(grad_query, 1, core), middle_got), 1, z)
    middle_arrived = send_ahead(middle_rows, "dz")
    middle_rows = total_of(middle_rows[0], *middle_arrived)
    middle_rows, kv_arrived = lax.optimization_barrier((middle_rows, kv_arrived))
    mine = kv_grad[0].astype(f32) + kv_arrived[0].astype(f32) + kv_arrived[1].astype(f32)
    kv_sum = mine[0] + move(mine[1].astype(bf16), dy=2).astype(f32)

    early = four_ahead(jnp.concatenate([early, middle_rows], 1), 1, x)
    early, kv_sum = lax.optimization_barrier((early, kv_sum))
    arrived = send_ahead(early, "dx")
    grad_kv, input_grad = finish(
        kv_sum, normed_one, weight_one, hidden, gains, middle_grad, normed_grad, grad_gain_two, cosine, sine
    )

    early = total_of(early[0], *arrived)
    own, other = part_of(early, 0, y_lo), part_of(early, 0, 1 - y_lo)
    grad_kv = grad_kv.reshape(2, 2, LATE, LANES)
    keep, away = part_of(grad_kv, 1, core), part_of(grad_kv, 1, 1 - core)
    own, other, away = lax.optimization_barrier((own, other, away))
    late_arrived = move(away, dc=1)
    arrived = send_over_y(own, other)
    late = total_of(keep, late_arrived)
    late_own, late_other = part_of(late, 0, y_lo), part_of(late, 0, 1 - y_lo)

    early = total_of(own, *arrived)
    early, late_own, late_other = lax.optimization_barrier((early, late_own, late_other))
    late_arrived = send_over_y(late_own, late_other)
    arrived = send_ahead([early] * 4, "dx")
    late = total_of(late_own, *late_arrived)

    early = in_order(early, arrived, x).reshape(CHUNK + MIDDLE // 4, LANES)
    early, late = lax.optimization_barrier((early, late))
    before, after = move(early, dz=1), move(early, dz=-1)
    late = total_of(late, *send_ahead([late] * 4, "dx"))
    before, after, late = lax.optimization_barrier((before, after, late))
    half = early.shape[0] // 2
    far_low, far_high = move(before[:half], dz=1), move(after[half:], dz=-1)
    late = total_of(late, *send_ahead([late] * 4, "dz"))
    grad_gate, grad_up, grad_down, grad_output, grad_query, grad_key, grad_value, gain_grads = unpack(
        info, early, before, after, far_low, far_high, late
    )
    return (
        hidden_out.T[None],
        input_grad.T[None],
        gain_grads[0],
        grad_query,
        grad_key,
        grad_value,
        grad_output,
        gain_grads[1],
        grad_gate,
        grad_up,
        grad_down.T,
    )


def solution(mesh):
    placed = (
        P(("dp", "shard"), "ctx", None),
        P("shard"),
        P("shard", None),
        P("shard", None),
        P("shard", None),
        P("shard", None),
        P("shard"),
        P("shard", None),
        P("shard", None),
        P("shard", None),
        P(("dp", "shard"), None),
        P(("dp", "shard"), "ctx", None),
    )
    return jax.shard_map(
        body,
        mesh=mesh,
        in_specs=placed,
        out_specs=(
            P(("dp", "shard"), "ctx", None),
            P(("dp", "shard"), "ctx", None),
            P("shard"),
            P("shard", None),
            P("shard", None),
            P("shard", None),
            P("shard", None),
            P("shard"),
            P("shard", None),
            P("shard", None),
            P("shard", None),
        ),
        check_vma=False,
    )
```

```python
import functools

import jax
import jax.numpy as jnp
from jax import lax
from jax.experimental import pallas as pl
from jax.experimental.pallas import tpu as pltpu
from jax.sharding import PartitionSpec as P

HEADS = 9
KV_HEADS = 3
GROUP = 3
HEAD = 64
WIDTH = 576
FF = 1536
SPAN = 384
HALF = 192
CYCLE = 8
BLOCKS = 2 * CYCLE
QUERIES = 640
LANES = 128
ROWS = 144
EARLY = 6144
CHUNK = EARLY // 4
MIDDLE = 768
LATE = 448
TAIL = 448
REST = 3 * FF + WIDTH + 64

eps_norm = 1e-05
rope_base = 100000.0
masked_score = -1e30
bf16 = jnp.bfloat16
f32 = jnp.float32
AXES = ("ctx", "dp", "shard")
VMEM_LIMIT = 56 * 1024 * 1024
SMEM = pl.BlockSpec(memory_space=pltpu.SMEM)
VMEM = pl.BlockSpec(memory_space=pltpu.VMEM)


def move(block, dx=0, dy=0, dz=0, dc=0):
    route = []
    for x in range(4):
        for y in range(4):
            for z in range(4):
                for core in range(2):
                    ends = []
                    for a, b, c, d in (
                        (x, y, z, core),
                        ((x + dx) % 4, (y + dy) % 4, (z + dz) % 4, (core + dc) % 2),
                    ):
                        ends.append(((a * 2 + b // 2) * 4 + c) * 4 + (b % 2) * 2 + d)
                    route.append(tuple(ends))
    return lax.ppermute(block, AXES, route)


def dot(left, right, dims):
    return lax.dot_general(left, right, (dims, ((), ())), preferred_element_type=f32)


NN = ((1,), (0,))
NT = ((1,), (1,))


def turned(array):
    return array.astype(f32).T.astype(bf16)


def lane_of(shape):
    return lax.broadcasted_iota(jnp.int32, shape, 1)


def tile_of(index):
    return slice(index * LANES, (index + 1) * LANES)


def swapped_halves(tile):
    lane = lane_of(tile.shape)
    return jnp.where(lane % HEAD < HEAD // 2, pltpu.roll(tile, LANES - 32, 1), pltpu.roll(tile, 32, 1))


def fetch_pair(first, second):
    first_other = move(first, dy=1)
    second_other = move(second, dy=-1)
    return (
        first, move(first, dc=1), first_other, move(first_other, dc=1),
        second, move(second, dc=1), second_other, move(second_other, dc=1),
    )


def spread_shards(me, parts, out, cut):
    own, low, high, core_own, core_low, core_high = parts
    out[me] = own[...]
    out[me ^ 1] = core_own[...]
    out[me ^ 2, :, :cut] = low[...]
    out[me ^ 2, :, cut:] = high[...]
    out[me ^ 3, :, :cut] = core_low[...]
    out[me ^ 3, :, cut:] = core_high[...]


def fetch_shards(own, cut):
    low = move(own[:, :cut], dy=1)
    high = move(own[:, cut:], dy=-1)
    return own, low, high, move(own, dc=1), move(low, dc=1), move(high, dc=1)


def project_kernel(info, hidden_ref, *refs):
    parts, (cos_ref, sin_ref, normed_ref, query_ref, kv_ref, weight_ref, gains_ref, tails) = refs[:8], refs[8:]
    me = info[BLOCKS + 1]
    for index in range(4):
        weight_ref[me ^ index, :, :WIDTH] = parts[index][...]
        tails[me ^ index] = parts[4 + index][...]
    tail = tails[...].reshape(WIDTH, TAIL).astype(f32)
    gains = tail[:, 3 * LANES :].T
    gains_ref[0] = gains[0:1]
    gains_ref[1] = gains[32:33]
    weight_ref[:, :, WIDTH:QUERIES] = jnp.zeros((4, ROWS, HEAD), bf16)
    for head in range(KV_HEADS):
        both = [tail[:, start : start + HEAD] for start in (head * HEAD, (KV_HEADS + head) * HEAD)]
        weight_ref[:, :, tile_of(5 + head)] = jnp.concatenate(both, 1).astype(bf16).reshape(4, ROWS, LANES)
    hidden = hidden_ref[...].astype(f32).T
    inverse = lax.rsqrt(jnp.mean(hidden * hidden, axis=-1, keepdims=True) + eps_norm)
    normed = (hidden * inverse * gains[0:1]).astype(bf16)
    normed_ref[...] = normed
    cosine = cos_ref[...]
    sine = sin_ref[...]
    first = lane_of((SPAN, LANES)) < HEAD
    for tile in range(8):
        raw = dot(normed, weight_ref[:, :, tile_of(tile)].reshape(WIDTH, LANES), NN)
        roped = raw * cosine + swapped_halves(raw) * sine
        if tile < 5:
            roped = roped * (HEAD**-0.5)
            query_ref[:, tile_of(2 * tile)] = jnp.where(first, roped, 0.0).astype(bf16)
            if tile < 4:
                query_ref[:, tile_of(2 * tile + 1)] = jnp.where(first, pltpu.roll(roped, HEAD, 1), 0.0).astype(bf16)
        else:
            kv_ref[:, tile_of(tile - 5)] = jnp.where(first, roped, raw).astype(bf16)


def project(info, hidden, parts, cosine, sine):
    return pl.pallas_call(
        project_kernel,
        out_shape=(
            jax.ShapeDtypeStruct((SPAN, WIDTH), bf16),
            jax.ShapeDtypeStruct((SPAN, HEADS * LANES), bf16),
            jax.ShapeDtypeStruct((SPAN, KV_HEADS * LANES), bf16),
            jax.ShapeDtypeStruct((4, ROWS, 1024), bf16),
            jax.ShapeDtypeStruct((2, 1, WIDTH), f32),
        ),
        in_specs=[SMEM] + [VMEM] * 11,
        scratch_shapes=[pltpu.VMEM((4, ROWS, TAIL), bf16)],
        compiler_params=pltpu.CompilerParams(vmem_limit_bytes=VMEM_LIMIT),
        cost_estimate=pl.CostEstimate(flops=2 * SPAN * WIDTH * 1024, bytes_accessed=4 << 20, transcendentals=0),
        name="project",
    )(info, hidden, *parts, cosine, sine)


def stacked_heads(ref, half, group):
    return jnp.concatenate(
        [ref[half * HALF : (half + 1) * HALF, tile_of(group * GROUP + head)] for head in range(GROUP)]
        + [jnp.zeros((QUERIES - GROUP * HALF, LANES), ref.dtype)],
        axis=0,
    )


def allowed_pairs():
    shape = (HALF, QUERIES)
    return lax.broadcasted_iota(jnp.int32, shape, 0) <= lane_of(shape) % HALF


def attend_kernel(info, query_ref, *refs):
    kv_parts, (mixed_ref, log_ref, kv_ref), scratch = refs[:10], refs[10:13], refs[13:]
    for index in range(6):
        for half in range(2):
            kv_ref[2 * index + half] = kv_parts[index][half * HALF : (half + 1) * HALF]
    for half in range(4):
        kv_ref[12 + half] = kv_parts[6 + half][...]
    query, summed, peak, total = (scratch[3 * i : 3 * i + 3] for i in range(4))
    groups = range(KV_HEADS)
    high = lane_of((QUERIES, LANES)) >= HEAD
    for half in range(2):
        for group in groups:
            query[group][...] = turned(stacked_heads(query_ref, half, group))
            summed[group][...] = jnp.zeros((HEAD, QUERIES), f32)
            peak[group][...] = jnp.full((1, QUERIES), masked_score, f32)
            total[group][...] = jnp.zeros((1, QUERIES), f32)

        def visit(place, diagonal):
            blocks = [kv_ref[place, :, tile_of(group)] for group in groups]
            scores = [dot(blocks[group], query[group][...], NN) for group in groups]
            for group in groups:
                masked = jnp.where(allowed_pairs(), scores[group], masked_score) if diagonal else scores[group]
                old_peak = peak[group][...]
                new_peak = jnp.maximum(old_peak, jnp.max(masked, axis=0, keepdims=True))
                raised = jnp.exp(masked - new_peak)
                factor = jnp.exp(old_peak - new_peak)
                peak[group][...] = new_peak
                total[group][...] = total[group][...] * factor + jnp.sum(raised, axis=0, keepdims=True)
                product = dot(turned(blocks[group])[HEAD:], raised.astype(bf16), NN)
                summed[group][...] = summed[group][...] * factor + product

        def step(index, carry):
            visit(info[index], False)
            return carry

        last = info[BLOCKS] if half == 0 else 2 * CYCLE - 1 - info[BLOCKS]
        lax.fori_loop(0, last, step, 0)
        visit(info[last], True)
        for group in groups:
            mixed = summed[group][...] / total[group][...]
            upright = jnp.concatenate([jnp.zeros((HEAD, QUERIES), f32), mixed], 0).T
            log_ref[half, group] = peak[group][...] + jnp.log(total[group][...])
            for head in range(GROUP):
                mixed_ref[half * HALF : (half + 1) * HALF, tile_of(group * GROUP + head)] = upright[
                    head * HALF : (head + 1) * HALF
                ]


def attend(info, query, kv_parts):
    return pl.pallas_call(
        attend_kernel,
        out_shape=(
            jax.ShapeDtypeStruct((SPAN, HEADS * LANES), f32),
            jax.ShapeDtypeStruct((2, KV_HEADS, 1, QUERIES), f32),
            jax.ShapeDtypeStruct((BLOCKS, HALF, KV_HEADS * LANES), bf16),
        ),
        in_specs=[SMEM] + [VMEM] * 11,
        scratch_shapes=[pltpu.VMEM((LANES, QUERIES), bf16)] * 3
        + [pltpu.VMEM((HEAD, QUERIES), f32)] * 3
        + [pltpu.VMEM((1, QUERIES), f32)] * 6,
        compiler_params=pltpu.CompilerParams(vmem_limit_bytes=VMEM_LIMIT),
        cost_estimate=pl.CostEstimate(flops=20 << 30, bytes_accessed=8 << 20, transcendentals=17 * HALF * QUERIES * 3),
        name="attend",
    )(info, query, *kv_parts)


def attend_back_kernel(
    info, query_ref, kv_ref, mixed_ref, mixed_grad_ref, log_ref, cos_ref, sin_ref, query_grad_ref, kv_grad_ref, *scratch
):
    query, query_t, grads, grads_t, query_sum, kv_sum, delta, log_total = (
        scratch[3 * i : 3 * i + 3] for i in range(8)
    )
    groups = range(KV_HEADS)
    for group in groups:
        kv_sum[group][...] = jnp.zeros((BLOCKS, HALF, LANES), f32)
    first = lane_of((HALF, LANES)) < HEAD
    for half in range(2):
        rows = slice(half * HALF, (half + 1) * HALF)
        for group in groups:
            stacked = stacked_heads(query_ref, half, group)
            query[group][...] = stacked
            query_t[group][...] = turned(stacked)
            stacked = stacked_heads(mixed_grad_ref, half, group)
            grads[group][...] = stacked
            grads_t[group][...] = turned(stacked)
            terms = stacked.astype(f32) * stacked_heads(mixed_ref, half, group)
            delta[group][...] = jnp.sum(terms.T, axis=0, keepdims=True)
            log_total[group][...] = log_ref[half, group]
            query_sum[group][...] = jnp.zeros((HEAD, QUERIES), f32)

        def visit(place, diagonal):
            blocks = [kv_ref[place, :, tile_of(group)] for group in groups]
            scores = [dot(blocks[group], query_t[group][...], NN) for group in groups]
            chance_grads = [dot(blocks[group], grads_t[group][...], NN) for group in groups]
            for group in groups:
                masked = jnp.where(allowed_pairs(), scores[group], masked_score) if diagonal else scores[group]
                chance = jnp.exp(masked - log_total[group][...])
                score_grad = (chance * (chance_grads[group] - delta[group][...])).astype(bf16)
                kv_sum[group][place] += dot(chance.astype(bf16), grads[group][...], NN) + dot(
                    score_grad, query[group][...], NN
                )
                query_sum[group][...] += dot(turned(blocks[group])[:HEAD], score_grad, NN)

        def step(index, carry):
            visit(info[index], False)
            return carry

        last = info[BLOCKS] if half == 0 else 2 * CYCLE - 1 - info[BLOCKS]
        lax.fori_loop(0, last, step, 0)
        visit(info[last], True)
        cosine = cos_ref[rows, :]
        sine = sin_ref[rows, :]
        for group in groups:
            upright = jnp.concatenate([query_sum[group][...], jnp.zeros((HEAD, QUERIES), f32)], 0).T
            for head in range(GROUP):
                tile = upright[head * HALF : (head + 1) * HALF] * (HEAD**-0.5)
                tile = tile * cosine - swapped_halves(tile) * sine
                query_grad_ref[rows, tile_of(group * GROUP + head)] = jnp.where(first, tile, 0.0).astype(bf16)
    for group in groups:
        kv_grad_ref[:, :, tile_of(group)] = kv_sum[group][...].astype(bf16)


def attend_back(info, query, kv, mixed, mixed_grad, log_total, cosine, sine):
    return pl.pallas_call(
        attend_back_kernel,
        out_shape=(
            jax.ShapeDtypeStruct((SPAN, HEADS * LANES), bf16),
            jax.ShapeDtypeStruct((BLOCKS, HALF, KV_HEADS * LANES), bf16),
        ),
        in_specs=[SMEM] + [VMEM] * 7,
        scratch_shapes=(
            [pltpu.VMEM((QUERIES, LANES), bf16)] * 3
            + [pltpu.VMEM((LANES, QUERIES), bf16)] * 3
            + [pltpu.VMEM((QUERIES, LANES), bf16)] * 3
            + [pltpu.VMEM((LANES, QUERIES), bf16)] * 3
            + [pltpu.VMEM((HEAD, QUERIES), f32)] * 3
            + [pltpu.VMEM((BLOCKS, HALF, LANES), f32)] * 3
            + [pltpu.VMEM((1, QUERIES), f32)] * 6
        ),
        compiler_params=pltpu.CompilerParams(vmem_limit_bytes=VMEM_LIMIT),
        cost_estimate=pl.CostEstimate(flops=40 << 30, bytes_accessed=12 << 20, transcendentals=17 * HALF * QUERIES * 3),
        name="attend_back",
    )(info, query, kv, mixed, mixed_grad, log_total, cosine, sine)


def feed_kernel(
    info, hidden_ref, cotangent_ref, mixed_ref, gains_ref, own, low, high, core_own, core_low, core_high,
    out_ref, middle_grad_ref, mixed_grad_ref, gain_grad_ref, keep_ref, away_ref, weight, grads_t, down, normed_t, attended_t,
):
    spread_shards(info[BLOCKS + 1], (own, low, high, core_own, core_low, core_high), weight, FF + FF)
    core = info[BLOCKS + 2]
    gain = gains_ref[1]

    def columns(start, width):
        return weight[:, :, start : start + width].reshape(WIDTH, width)

    weight_output = columns(3 * FF, WIDTH)
    for shard in range(4):
        for part in range(4):
            start = 2 * FF + part * SPAN
            down[part * ROWS : (part + 1) * ROWS, shard * SPAN : (shard + 1) * SPAN] = weight[shard, :, start : start + SPAN]

    def store(ref, y, start, value):
        done = 0
        while done < value.shape[0]:
            chunk, within = divmod(start + done, CHUNK)
            count = min(value.shape[0] - done, CHUNK - within)
            ref[chunk, y, within : within + count, :] = value[done : done + count, :]
            done += count

    def store_ordered(tile, value):
        for k in range(4):
            store(keep_ref if k < 2 else away_ref, k % 2, tile * ROWS, value[k * ROWS : (k + 1) * ROWS, :])

    tiles = []
    for tile in range(5):
        joined = pltpu.roll(mixed_ref[:, tile_of(2 * tile)], HEAD, 1)
        if tile < 4:
            joined = joined + mixed_ref[:, tile_of(2 * tile + 1)]
        tiles.append(joined)
    attended = jnp.concatenate(tiles, 1)
    attended_t[...] = attended.T.astype(bf16)
    attended = attended[:, :WIDTH].astype(bf16)
    middle = hidden_ref[...].astype(f32).T + dot(attended, weight_output, NN)
    inverse = lax.rsqrt(jnp.mean(middle * middle, axis=-1, keepdims=True) + eps_norm)
    normed_wide = middle * inverse * gain
    normed = normed_wide.astype(bf16)
    normed_t[...] = normed_wide.T.astype(bf16)

    def keep_first(ref):
        starts = [(2 * (k % 2) + (core if k < 2 else 1 - core)) * ROWS for k in range(4)]
        return jnp.concatenate([ref[pl.ds(pl.multiple_of(start, 16), ROWS), :] for start in starts], 0)

    normed_rows = keep_first(normed_t)
    attended_rows = keep_first(attended_t)
    cotangent_t = cotangent_ref[...]
    grads_t[...] = turned(cotangent_t)
    branch_grad = grads_t[...]

    total = middle
    normed_grad = jnp.zeros((SPAN, WIDTH), f32)
    for part in range(3):
        weight_gate = columns(part * 512, 512)
        weight_up = columns(FF + part * 512, 512)
        weight_down = down[:, part * 512 : (part + 1) * 512]
        gate = dot(normed, weight_gate, NN)
        lifted = dot(normed, weight_up, NN)
        act_grad = dot(branch_grad, weight_down, NN)
        sigmoid = 1.0 / (1.0 + jnp.exp(-gate))
        swish = gate * sigmoid
        activated = (swish * lifted).astype(bf16)
        total = total + dot(activated, weight_down, NT)
        gate_grad = (act_grad * lifted * sigmoid * (1.0 + gate * (1.0 - sigmoid))).astype(bf16)
        lifted_grad = (act_grad * swish).astype(bf16)
        normed_grad = normed_grad + dot(gate_grad, weight_gate, NT) + dot(lifted_grad, weight_up, NT)
        for base, upper in ((0, gate_grad), (12, lifted_grad)):
            grad = dot(normed_rows, upper, NN).astype(bf16)
            for tile in range(4):
                store_ordered(base + 4 * part + tile, grad[:, tile_of(tile)])
        grad = dot(cotangent_t, activated, NN).astype(bf16)
        for tile in range(4):
            shard, within = divmod(4 * part + tile, 3)
            for ref, here in ((keep_ref, core == shard % 2), (away_ref, core != shard % 2)):

                @pl.when(here)
                def _(ref=ref):
                    store(ref, shard // 2, 24 * ROWS + within * WIDTH, grad[:, tile_of(tile)])

    out_ref[...] = total.T.astype(bf16)
    scaled = normed_grad * gain
    gain_grad_ref[...] = jnp.sum(normed_grad * middle * inverse, axis=0, keepdims=True)
    middle_grad = (
        branch_grad.astype(f32)
        + inverse * scaled
        - inverse * inverse * inverse * middle * jnp.mean(scaled * middle, axis=-1, keepdims=True)
    )
    middle_grad_ref[...] = middle_grad
    block_grad = middle_grad.astype(bf16)
    grad = dot(attended_rows, block_grad, NN).astype(bf16)
    grad = jnp.concatenate([grad, jnp.zeros((WIDTH, 64), bf16)], 1)
    for tile in range(5):
        store_ordered(36 + tile, grad[:, tile_of(tile)])
    for ref in (keep_ref, away_ref):
        ref[3, :, 41 * ROWS - 3 * CHUNK :, :] = jnp.zeros((2, EARLY - 41 * ROWS, LANES), bf16)
    mixed_grad = dot(block_grad, weight_output, NT)
    mixed_grad = jnp.concatenate([mixed_grad, jnp.zeros((SPAN, 64), f32)], 1)
    second = lane_of((SPAN, LANES)) >= HEAD
    for tile in range(5):
        both = mixed_grad[:, tile_of(tile)]
        mixed_grad_ref[:, tile_of(2 * tile)] = jnp.where(second, pltpu.roll(both, HEAD, 1), 0.0).astype(bf16)
        if tile < 4:
            mixed_grad_ref[:, tile_of(2 * tile + 1)] = jnp.where(second, both, 0.0).astype(bf16)


def feed(info, hidden, cotangent, mixed, gains, parts):
    return pl.pallas_call(
        feed_kernel,
        out_shape=(
            jax.ShapeDtypeStruct((WIDTH, SPAN), bf16),
            jax.ShapeDtypeStruct((SPAN, WIDTH), f32),
            jax.ShapeDtypeStruct((SPAN, HEADS * LANES), bf16),
            jax.ShapeDtypeStruct((1, WIDTH), f32),
            jax.ShapeDtypeStruct((4, 2, CHUNK, LANES), bf16),
            jax.ShapeDtypeStruct((4, 2, CHUNK, LANES), bf16),
        ),
        in_specs=[SMEM] + [VMEM] * 10,
        scratch_shapes=[
            pltpu.VMEM((4, ROWS, REST), bf16),
            pltpu.VMEM((SPAN, WIDTH), bf16),
            pltpu.VMEM((WIDTH, FF), bf16),
            pltpu.VMEM((WIDTH, SPAN), bf16),
            pltpu.VMEM((QUERIES, SPAN), bf16),
        ],
        compiler_params=pltpu.CompilerParams(vmem_limit_bytes=VMEM_LIMIT),
        cost_estimate=pl.CostEstimate(flops=8 << 30, bytes_accessed=20 << 20, transcendentals=SPAN * FF),
        name="feed",
    )(info, hidden, cotangent, mixed, gains, *parts)


def store_grads(ref, normed_t, before, tiles):
    for tile in range(tiles):
        part = dot(normed_t, before[:, tile_of(tile)], NN).astype(bf16)
        for shard in range(4):
            ref[shard, tile * ROWS : (tile + 1) * ROWS, :] = part[shard * ROWS : (shard + 1) * ROWS, :]


def query_back_kernel(query_grad_ref, normed_ref, weight_ref, weight_grad_ref, normed_grad_ref, pre):
    for tile in range(5):
        joined = query_grad_ref[:, tile_of(2 * tile)].astype(f32)
        if tile < 4:
            joined = joined + pltpu.roll(query_grad_ref[:, tile_of(2 * tile + 1)].astype(f32), HEAD, 1)
        pre[:, tile_of(tile)] = joined.astype(bf16)
    before = pre[...]
    store_grads(weight_grad_ref, turned(normed_ref[...]), before, 5)
    weight_grad_ref[:, 5 * ROWS :, :] = jnp.zeros((4, MIDDLE - 5 * ROWS, LANES), bf16)
    normed_grad_ref[...] = dot(before, weight_ref[:, :, :QUERIES].reshape(WIDTH, QUERIES), NT)


def query_back(query_grad, normed, weight):
    return pl.pallas_call(
        query_back_kernel,
        out_shape=(
            jax.ShapeDtypeStruct((4, MIDDLE, LANES), bf16),
            jax.ShapeDtypeStruct((SPAN, WIDTH), f32),
        ),
        in_specs=[VMEM] * 3,
        scratch_shapes=[pltpu.VMEM((SPAN, QUERIES), bf16)],
        compiler_params=pltpu.CompilerParams(vmem_limit_bytes=VMEM_LIMIT),
        cost_estimate=pl.CostEstimate(flops=4 * SPAN * WIDTH * QUERIES, bytes_accessed=4 << 20, transcendentals=0),
        name="query_back",
    )(query_grad, normed, weight)


def finish_kernel(
    kv_sum_ref, normed_ref, weight_ref, hidden_ref, gains_ref, middle_grad_ref, normed_grad_ref, gain_grad_ref,
    cos_ref, sin_ref, weight_grad_ref, input_grad_ref, pre,
):
    cosine = cos_ref[...]
    sine = sin_ref[...]
    first = lane_of((SPAN, LANES)) < HEAD
    for tile in range(3):
        raw = kv_sum_ref[:, tile_of(tile)]
        back = raw * cosine - swapped_halves(raw) * sine
        pre[:, tile_of(tile)] = jnp.where(first, back, raw).astype(bf16)
    before = pre[...]
    store_grads(weight_grad_ref, turned(normed_ref[...]), before, 3)
    normed_grad = normed_grad_ref[...] + dot(before, weight_ref[:, :, QUERIES:].reshape(WIDTH, 3 * LANES), NT)
    hidden = hidden_ref[...].astype(f32).T
    inverse = lax.rsqrt(jnp.mean(hidden * hidden, axis=-1, keepdims=True) + eps_norm)
    scaled = normed_grad * gains_ref[0]
    first_gain_grad = jnp.sum(normed_grad * hidden * inverse, axis=0, keepdims=True)
    gain_grads = jnp.concatenate([first_gain_grad, gain_grad_ref[...]], 0)
    gain_grads = jnp.concatenate([gain_grads, jnp.zeros((2, WIDTH), f32)], 0)
    weight_grad_ref[:, 3 * ROWS :, :] = jnp.zeros((4, LATE - 3 * ROWS, LANES), bf16)
    for shard in range(4):
        part = gain_grads[:, shard * ROWS : (shard + 1) * ROWS]
        rest = jnp.concatenate([part[:, LANES:], jnp.zeros((4, LANES - (ROWS - LANES)), f32)], 1)
        rows = jnp.concatenate([part[:, :LANES], rest, jnp.zeros((8, LANES), f32)], 0)
        weight_grad_ref[shard, 3 * ROWS : 3 * ROWS + 16, :] = rows.astype(bf16)
    input_grad = (
        middle_grad_ref[...]
        + inverse * scaled
        - inverse * inverse * inverse * hidden * jnp.mean(scaled * hidden, axis=-1, keepdims=True)
    )
    input_grad_ref[...] = input_grad.T


def finish(*operands):
    return pl.pallas_call(
        finish_kernel,
        out_shape=(
            jax.ShapeDtypeStruct((4, LATE, LANES), bf16),
            jax.ShapeDtypeStruct((WIDTH, SPAN), f32),
        ),
        in_specs=[VMEM] * 10,
        scratch_shapes=[pltpu.VMEM((SPAN, 3 * LANES), bf16)],
        compiler_params=pltpu.CompilerParams(vmem_limit_bytes=VMEM_LIMIT),
        cost_estimate=pl.CostEstimate(flops=4 * SPAN * WIDTH * SPAN, bytes_accessed=8 << 20, transcendentals=0),
        name="finish",
    )(*operands)


def total_of(*blocks):
    total = blocks[0].astype(f32)
    for block in blocks[1:]:
        total = total + block.astype(f32)
    return total.astype(bf16)


def four_ahead(array, dim, here):
    size = array.shape[dim] // 4
    return [lax.dynamic_slice_in_dim(array, ((here + step) % 4) * size, size, dim) for step in range(4)]


def send_ahead(blocks, axis):
    return [move(blocks[step], **{axis: step}) for step in (1, 3, 2)]


def send_over_y(own, other):
    return [move(other, dy=1), move(other, dy=3), move(own, dy=2)]


def in_order(own, arrived, here):
    before, after, far = arrived
    around = jnp.stack([own, after, far, before], 0)
    return jnp.concatenate([lax.dynamic_slice_in_dim(around, (step - here) % 4, 1, 0) for step in range(4)], 0)


def part_of(rows, dim, index):
    return lax.dynamic_slice_in_dim(rows, index, 1, dim).reshape(rows.shape[:dim] + rows.shape[dim + 1 :])


def unpack_kernel(
    info, own, before, after, far_low, far_high, late,
    gate_ref, up_ref, down_ref, output_ref, query_ref, key_ref, value_ref, gains_ref, rows,
):
    z = info[BLOCKS + 3]
    half = far_low.shape[0]
    rows[z] = own[...]
    rows[(z + 3) % 4] = before[...]
    rows[(z + 1) % 4] = after[...]
    rows[(z + 2) % 4, :half] = far_low[...]
    rows[(z + 2) % 4, half:] = far_high[...]

    def fetch(start, count, size=CHUNK, base=0):
        parts = []
        while count:
            chunk, within = divmod(start, size)
            taken = min(count, size - within)
            parts.append(rows[chunk, base + within : base + within + taken, :].astype(f32))
            start, count = start + taken, count - taken
        return jnp.concatenate(parts, 0)

    for tile in range(12):
        gate_ref[:, tile_of(tile)] = fetch(tile * ROWS, ROWS)
        up_ref[:, tile_of(tile)] = fetch((12 + tile) * ROWS, ROWS)
    for tile in range(3):
        down_ref[:, tile_of(tile)] = fetch(24 * ROWS + tile * WIDTH, WIDTH)
    for tile in range(5):
        columns = slice(tile * LANES, min((tile + 1) * LANES, WIDTH))
        width = columns.stop - columns.start
        output_ref[:, columns] = fetch((36 + tile) * ROWS, ROWS)[:, :width]
        query_ref[:, columns] = fetch(tile * ROWS, ROWS, MIDDLE // 4, CHUNK)[:, :width]
    for head in range(KV_HEADS):
        both = late[head * ROWS : (head + 1) * ROWS, :].astype(f32)
        key_ref[:, head * HEAD : (head + 1) * HEAD] = both[:, :HEAD]
        value_ref[:, head * HEAD : (head + 1) * HEAD] = both[:, HEAD:]
    gains = late[3 * ROWS :, :].astype(f32)
    for index in range(2):
        gains_ref[index : index + 1, :LANES] = gains[index : index + 1]
        gains_ref[index : index + 1, LANES:] = gains[4 + index : 5 + index, : ROWS - LANES]


def unpack(*operands):
    shapes = ((ROWS, FF), (ROWS, FF), (WIDTH, SPAN), (ROWS, WIDTH), (ROWS, WIDTH), (ROWS, 192), (ROWS, 192), (2, ROWS))
    return pl.pallas_call(
        unpack_kernel,
        out_shape=tuple(jax.ShapeDtypeStruct(shape, f32) for shape in shapes),
        in_specs=[SMEM] + [VMEM] * 6,
        scratch_shapes=[pltpu.VMEM((4, CHUNK + MIDDLE // 4, LANES), bf16)],
        compiler_params=pltpu.CompilerParams(vmem_limit_bytes=VMEM_LIMIT),
        cost_estimate=pl.CostEstimate(flops=0, bytes_accessed=6 << 20, transcendentals=0),
        name="unpack",
    )(*operands)


def body(
    hidden_in,
    first_gain,
    query_weight,
    key_weight,
    value_weight,
    output_weight,
    second_gain,
    gate_weight,
    up_weight,
    down_weight,
    pair_slot,
    out_cotangent,
):
    cycle_index = lax.axis_index("ctx")
    x = cycle_index // 2
    y_hi = cycle_index % 2
    z = lax.axis_index("dp")
    me = lax.axis_index("shard")
    y_lo = me // 2
    core = me % 2
    slots = pair_slot[0]

    gains = jnp.concatenate(
        [jnp.broadcast_to(first_gain[:, None], (ROWS, 32)), jnp.broadcast_to(second_gain[:, None], (ROWS, 32))], 1
    )
    packed = fetch_pair(query_weight, jnp.concatenate([key_weight, value_weight, gains], 1))

    owners = jnp.arange(CYCLE, dtype=jnp.int32)
    slot = jnp.sum(jnp.where(owners == cycle_index, slots, 0))
    row = lax.broadcasted_iota(jnp.int32, (SPAN, LANES), 0)
    lane = lax.broadcasted_iota(jnp.int32, (SPAN, LANES), 1)
    place = jnp.where(row < HALF, slot, 2 * CYCLE - 1 - slot) * HALF + row % HALF
    freqs = rope_base ** (-(2 * (jnp.arange(LANES) % 32)).astype(f32) / HEAD)
    angles = place.astype(f32) * freqs[None, :]
    cosine = jnp.cos(angles)
    sine = jnp.where(lane % HEAD < HEAD // 2, -1.0, 1.0) * jnp.sin(angles)

    steps = jnp.array([0, 0, 3, 3, 1, 1, 2, 2], jnp.int32)
    there = ((x + steps) % 4) * 2 + (y_hi + owners) % 2
    found = jnp.sum(jnp.where(there[:, None] == owners[None, :], slots[None, :], 0), 1)
    order = jnp.arange(BLOCKS, dtype=jnp.int32)
    where_found = jnp.sum(
        jnp.where(found[None, :] == order[:, None], 2 * owners[None, :], 0)
        + jnp.where(BLOCKS - 1 - found[None, :] == order[:, None], 2 * owners[None, :] + 1, 0),
        1,
    )
    info = jnp.concatenate([where_found, slot[None], me[None], core[None], z[None]]).astype(jnp.int32)

    hidden = hidden_in[0].T
    cotangent = out_cotangent[0].T
    normed_one, query, kv_own, weight_one, gains = project(info, hidden, packed, cosine, sine)

    partner = move(kv_own, dy=2)
    left = move(kv_own, dx=1)
    right = move(kv_own, dx=-1)
    rest = jnp.concatenate(
        [gate_weight, up_weight, down_weight.T.reshape(4, ROWS, SPAN)[0]]
        + [down_weight.T.reshape(4, ROWS, SPAN)[part] for part in (1, 2, 3)]
        + [output_weight, jnp.zeros((ROWS, 64), bf16)],
        1,
    )
    rest, partner, left, right = lax.optimization_barrier((rest, partner, left, right))
    rest = fetch_shards(rest, FF + FF)
    left_partner = move(partner, dx=1)
    right_partner = move(partner, dx=-1)
    far = [move(left[:HALF], dx=1), move(right[HALF:], dx=-1)]
    far_partner = [move(left_partner[:HALF], dx=1), move(right_partner[HALF:], dx=-1)]
    mixed, log_total, kv = attend(
        info, query, [kv_own, partner, left, left_partner, right, right_partner] + far + far_partner
    )
    hidden_out, middle_grad, mixed_grad, grad_gain_two, keep, away = feed(info, hidden, cotangent, mixed, gains, rest)
    got = move(away, dc=1)

    query_grad, kv_grad = attend_back(info, query, kv, mixed, mixed_grad, log_total, cosine, sine)
    kv_grad = kv_grad.reshape(4, 2, SPAN, KV_HEADS * LANES)
    far_low, far_high = kv_grad[3, :, :HALF], kv_grad[3, :, HALF:]
    far_low, far_high, query_grad = lax.optimization_barrier((far_low, far_high, query_grad))
    from_left = move(far_low, dx=1)
    from_right = move(far_high, dx=-1)

    early, query_grad = lax.optimization_barrier((total_of(keep, got), query_grad))
    early = lax.psum_scatter(early, "dp", scatter_dimension=0, tiled=False)
    grad_query, normed_grad = query_back(query_grad, normed_one, weight_one)
    grad_query = grad_query.reshape(2, 2, MIDDLE, LANES)
    middle_got = move(part_of(grad_query, 1, 1 - core), dc=1)

    to_left = jnp.concatenate([kv_grad[1, :, :HALF], kv_grad[1, :, HALF:] + from_right], 1)
    to_right = jnp.concatenate([kv_grad[2, :, :HALF] + from_left, kv_grad[2, :, HALF:]], 1)
    to_left, to_right, middle_got = lax.optimization_barrier((to_left, to_right, middle_got))
    kv_arrived = move(to_right, dx=1), move(to_left, dx=-1)
    middle_rows = four_ahead(total_of(part_of(grad_query, 1, core), middle_got), 1, z)
    middle_arrived = send_ahead(middle_rows, "dz")
    middle_rows = total_of(middle_rows[0], *middle_arrived)
    mine = kv_grad[0].astype(f32) + kv_arrived[0].astype(f32) + kv_arrived[1].astype(f32)
    kv_sum = mine[0] + move(mine[1].astype(bf16), dy=2).astype(f32)

    early = four_ahead(jnp.concatenate([early, middle_rows], 1), 1, x)
    early, kv_sum = lax.optimization_barrier((early, kv_sum))
    arrived = send_ahead(early, "dx")
    grad_kv, input_grad = finish(
        kv_sum, normed_one, weight_one, hidden, gains, middle_grad, normed_grad, grad_gain_two, cosine, sine
    )

    early = total_of(early[0], *arrived)
    own, other = part_of(early, 0, y_lo), part_of(early, 0, 1 - y_lo)
    grad_kv = grad_kv.reshape(2, 2, LATE, LANES)
    keep, away = part_of(grad_kv, 1, core), part_of(grad_kv, 1, 1 - core)
    own, other, away = lax.optimization_barrier((own, other, away))
    late_arrived = move(away, dc=1)
    arrived = send_over_y(own, other)
    late = total_of(keep, late_arrived)
    late_own, late_other = part_of(late, 0, y_lo), part_of(late, 0, 1 - y_lo)

    early = total_of(own, *arrived)
    early, late_own, late_other = lax.optimization_barrier((early, late_own, late_other))
    late_arrived = send_over_y(late_own, late_other)
    arrived = send_ahead([early] * 4, "dx")
    late = total_of(late_own, *late_arrived)

    early = in_order(early, arrived, x).reshape(CHUNK + MIDDLE // 4, LANES)
    early, late = lax.optimization_barrier((early, late))
    before, after = move(early, dz=1), move(early, dz=-1)
    late = total_of(late, *send_ahead([late] * 4, "dx"))
    before, after, late = lax.optimization_barrier((before, after, late))
    half = early.shape[0] // 2
    far_low, far_high, late = lax.optimization_barrier((before[:half], after[half:], late))
    far_low, far_high = move(far_low, dz=1), move(far_high, dz=-1)
    late = total_of(late, *send_ahead([late] * 4, "dz"))
    grad_gate, grad_up, grad_down, grad_output, grad_query, grad_key, grad_value, gain_grads = unpack(
        info, early, before, after, far_low, far_high, late
    )
    return (
        hidden_out.T[None],
        input_grad.T[None],
        gain_grads[0],
        grad_query,
        grad_key,
        grad_value,
        grad_output,
        gain_grads[1],
        grad_gate,
        grad_up,
        grad_down.T,
    )


def solution(mesh):
    placed = (
        P(("dp", "shard"), "ctx", None),
        P("shard"),
        P("shard", None),
        P("shard", None),
        P("shard", None),
        P("shard", None),
        P("shard"),
        P("shard", None),
        P("shard", None),
        P("shard", None),
        P(("dp", "shard"), None),
        P(("dp", "shard"), "ctx", None),
    )
    return jax.shard_map(
        body,
        mesh=mesh,
        in_specs=placed,
        out_specs=(
            P(("dp", "shard"), "ctx", None),
            P(("dp", "shard"), "ctx", None),
            P("shard"),
            P("shard", None),
            P("shard", None),
            P("shard", None),
            P("shard", None),
            P("shard"),
            P("shard", None),
            P("shard", None),
            P("shard", None),
        ),
        check_vma=False,
    )
```
